256 devices in a mesh: blk: 4 (over x), team: 4 (over y), dp: 16 (over z, core).
Axes of the slice: x: 4, y: 4, z: 8, core: 2. Of those that a mesh axis runs over, the one named last changes fastest.
Arguments:
- hidden: bfloat16 [8192, 28672], P(('blk', 'dp'), 'team'), may hold values from -6 to 6
- out_grad: bfloat16 [8192, 8192], P(('blk', 'dp'), 'team'), may hold values from -0.0625 to 0.0625
- act_rows: int32 [4, 64, 12], P('team'), may hold values from 0 to 55, as said below
- col_owner: int32 [64], replicated, may hold values from 0 to 3, as said below
Outputs:
- gradients: float32 [4, 4, 288, 128, 128], P('team', 'blk', 'dp')
- scores: float32 [4, 4, 288], P('team', 'blk', 'dp')
The draws below stay inside these ranges and needn't reach their ends.
Inputs may be any that keep to these rules, and one draw needn't show every extreme that they name: For each t and c the 12 entries act_rows[t, c, :] are distinct. `col_owner`: some owner holds exactly 24 block columns and no owner holds more.
All inputs are finite; a program needn't handle non-finite values.
Results may differ from the reference program's by a relative error of at most 0.0003.
Values may be sent and summed in bfloat16 or wider, within the bound.
No kernel may reach another device: no remote copies, remote signals or barrier semaphores. Data moves between devices by JAX's collectives and lax.ppermute only.
A program may use at most 192 MiB of HBM per device.

```python
import jax
import jax.numpy as jnp
from jax import lax

D = 8192
FF = 28672
BS = 128
KC = 12
DB = 64
FBT = 56
CAPC = 24
CAP = 288
TOKENS = 8192
N_BLK = 4
N_TEAM = 4


def draw_act_rows(key, part):
    key_list = jax.random.split(key, N_TEAM * DB)
    chosen = jax.vmap(lambda subkey: jax.random.permutation(subkey, FBT)[:KC])(key_list)
    return chosen.reshape(N_TEAM, DB, KC).astype(jnp.int32)


def draw_col_owner(key, part):
    first_key, second_key = jax.random.split(jax.random.fold_in(key, 7))
    shuffle = jax.random.permutation(first_key, DB)
    busiest = jax.random.randint(second_key, (), 0, N_BLK)
    position = jnp.arange(DB, dtype=jnp.int32)
    others = (position - CAPC) % (N_BLK - 1)
    others = others + (others >= busiest).astype(jnp.int32)
    values = jnp.where(position < CAPC, busiest, others).astype(jnp.int32)
    return jnp.zeros((DB,), jnp.int32).at[shuffle].set(values)


def block_levels(stream_key, shape, cuts, smallest, top_value):
    factor_of, own = 1.0, jax.random.fold_in(stream_key, 6)
    for axis_at, parts in cuts:
        heights = jnp.exp(jax.random.uniform(jax.random.fold_in(own, axis_at), (parts,), jnp.float32, smallest / len(cuts), top_value / len(cuts)))
        factor_of = factor_of * jnp.repeat(heights, shape[axis_at] // parts).reshape([-1 if axis == axis_at else 1 for axis in range(len(shape))])
    return factor_of


def centred(rng, dims, spread, bound, shards=(), kind=jnp.bfloat16):
    loudness = block_levels(rng, dims, shards, -0.22, 0.18) if shards else 1.0
    array = jax.random.normal(rng, dims, jnp.float32) * spread * loudness
    return jnp.minimum(jnp.maximum(array, -bound), bound).astype(kind)


def setup_inputs(seed: int = 0) -> dict:
    seeds = jax.random.split(jax.random.key(seed), 5)
    hidden = centred(seeds[0], (TOKENS, FF), 1.0, 6.0, ((0, 64), (1, 4)))
    out_grad = centred(seeds[1], (TOKENS, D), (TOKENS ** -0.5), 0.0625, ((0, 64), (1, 4)))
    act_rows = draw_act_rows(jax.random.fold_in(seeds[4], 71), 0)
    col_owner = draw_col_owner(jax.random.fold_in(seeds[4], 71), 0)
    return {"hidden": hidden, "out_grad": out_grad, "act_rows": act_rows, "col_owner": col_owner}


epsilon = 1e-06

def owner_tables(col_owner):
    owners = jnp.arange(N_BLK, dtype=jnp.int32)
    onehot = (col_owner[:, None] == owners[None, :]).astype(jnp.int32)
    column_rank = lax.optimization_barrier(jnp.sum((jnp.cumsum(onehot, axis=0) - onehot) * onehot, axis=1))
    slot_ids = jnp.arange(CAPC, dtype=jnp.int32)
    matches = (col_owner[None, None, :] == owners[:, None, None]) & (column_rank[None, None, :] == slot_ids[None, :, None])
    owned_columns = lax.optimization_barrier(jnp.sum(matches.astype(jnp.int32) * jnp.arange(DB, dtype=jnp.int32)[None, None, :], axis=2))
    alive_mask = jnp.any(matches, axis=2)
    return (owned_columns, alive_mask)

def reference(hidden, out_grad, act_rows, col_owner):
    owned_columns, alive_mask = owner_tables(col_owner)
    team_width = FF // N_TEAM
    grad_blocks = out_grad.reshape(TOKENS, DB, BS)

    def one_owner(position):
        team_index = position // N_BLK
        owner_index = position % N_BLK
        team_hidden = lax.dynamic_slice_in_dim(hidden, (team_index * team_width).astype(jnp.int32), team_width, 1)
        team_hidden = team_hidden.reshape(TOKENS, FBT, BS)
        chosen = owned_columns[owner_index]
        living = alive_mask[owner_index]
        block_rows = act_rows[team_index][chosen]
        picked_hidden = jnp.take(team_hidden, block_rows.reshape(-1), axis=1).reshape(TOKENS, CAPC, KC, BS).astype(jnp.float32)
        picked_grad = jnp.take(grad_blocks, chosen, axis=1).astype(jnp.float32)
        blocks = jnp.einsum('ncki,ncj->ckij', picked_hidden, picked_grad)
        blocks = blocks * living.astype(jnp.float32)[:, None, None, None]
        return blocks.reshape(CAP, BS, BS)
    gradients = lax.map(one_owner, jnp.arange(N_TEAM * N_BLK, dtype=jnp.int32))
    gradients = gradients.reshape(N_TEAM, N_BLK, CAP, BS, BS)
    scores = jnp.sqrt(lax.optimization_barrier(jnp.mean(gradients * gradients, axis=(3, 4))) + epsilon)
    return (gradients, scores)
```

```python
import functools

import jax
import jax.numpy as jnp
from jax import lax
from jax.experimental import pallas as pl
from jax.experimental.pallas import tpu as pltpu
from jax.sharding import PartitionSpec as P

BS = 128
NX, NZ = 4, 8
CAPC, KC, DB = 24, 12, 64
EPS = 1e-06
F32, BF16, I32 = jnp.float32, jnp.bfloat16, jnp.int32
OFFS = (4, 3, 2, 1, 0, -1, -2, -3)
VMEM = pl.BlockSpec(memory_space=pltpu.VMEM)
SMEM = pl.BlockSpec(memory_space=pltpu.SMEM)
ANY = pl.BlockSpec(memory_space=pl.ANY)


def perm(x, axis, n, step):
    return lax.ppermute(x, axis, [(i, (i + step) % n) for i in range(n)])


def x_right(v):
    return perm(v, "blk", NX, 1)


def x_left(v):
    return perm(v, "blk", NX, -1)


def z_right(v):
    return perm(v, "dp", 2 * NZ, 2)


def z_left(v):
    return perm(v, "dp", 2 * NZ, -2)


def other_core(v):
    return lax.ppermute(v, "dp", [(i, i ^ 1) for i in range(2 * NZ)])


def pick_kernel(cols, live, g, r0, l0, o0, r1, l1, o1):
    half = 64

    def put(e, s, ref, lane, row, lo, hi):
        c = cols[e * CAPC + s]
        a = live[e * CAPC + s]
        v = g[c // 16, lo:hi, pl.ds(pl.multiple_of((c % 16) * BS, BS), BS)]
        ref[row : row + hi - lo, lane * BS : (lane + 1) * BS] = jnp.where(a > 0, v, jnp.zeros_like(v))

    for s in range(CAPC):
        if s < 8:
            r, l, o, lane = r0, l0, o0, s
        else:
            r, l, o, lane = r1, l1, o1, s - 8
        put(0, s, r, lane, 0, 0, 128)
        put(2, s, r, lane, 128, 0, half)
        put(1, s, l, lane, 0, 0, 128)
        put(2, s, l, lane, 128, half, 128)
        put(3, s, o, lane, 0, 0, 128)


def pick(cols, live, g):
    shapes = []
    for n in (8, 16):
        shapes += [(192, n * BS), (192, n * BS), (128, n * BS)]
    return pl.pallas_call(
        pick_kernel,
        out_shape=[jax.ShapeDtypeStruct(s, BF16) for s in shapes],
        in_specs=[SMEM, SMEM, VMEM],
        out_specs=[VMEM] * 6,
        compiler_params=pltpu.CompilerParams(vmem_limit_bytes=32 * 2**20),
        name="pick_columns",
    )(cols, live, g)


def gemm_kernel(n, nh, rows, *refs):
    hs, gs = refs[:nh], refs[nh : nh + 2]
    outs = refs[nh + 2 : nh + 2 + len(OFFS)]
    hv = refs[nh + 2 + len(OFFS) : -1]
    sems = refs[-1]
    copies = [pltpu.make_async_copy(h, v, sems.at[i]) for i, (h, v) in enumerate(zip(hs, hv))]
    for c in copies:
        c.start()
    for c in copies:
        c.wait()
    for k in range(len(OFFS)):
        g = jnp.concatenate([gr[:, k * BS : (k + 1) * BS] for gr in gs], axis=0)

        def one(i, _, k=k, g=g):
            r = pl.multiple_of(rows[k * n + i] * BS, BS)
            h = jnp.concatenate([v[:, pl.ds(r, BS)] for v in hv], axis=0)
            outs[k][i] = lax.dot_general(h, g, (((0,), (0,)), ((), ())), preferred_element_type=F32)
            return 0

        lax.fori_loop(0, n, one, 0, unroll=True)


def gemm(n, rows, hs, gs):
    outs = [jax.ShapeDtypeStruct((n, BS, BS), F32)] * len(OFFS)
    tokens = sum(h.shape[0] for h in hs)
    return pl.pallas_call(
        functools.partial(gemm_kernel, n, len(hs)),
        out_shape=outs,
        in_specs=[SMEM] + [ANY] * len(hs) + [VMEM] * len(gs),
        out_specs=[VMEM] * len(OFFS),
        scratch_shapes=[pltpu.VMEM(h.shape, BF16) for h in hs] + [pltpu.SemaphoreType.DMA((len(hs),))],
        compiler_params=pltpu.CompilerParams(vmem_limit_bytes=50 * 2**20),
        cost_estimate=pl.CostEstimate(
            flops=2 * len(OFFS) * n * tokens * BS * BS, bytes_accessed=tokens * 7168 * 2, transcendentals=0
        ),
        name="block_products",
    )(rows, *hs, *gs)


def ring_sum(parts, right, left):
    p = dict(zip(OFFS, parts))
    p[-4] = p[4]
    m, q = p[right], p[-left]
    for k in range(right, 0, -1):
        m = z_right(m)
        if k > 1:
            m = m + p[k - 1]
    for k in range(left, 0, -1):
        q = z_left(q)
        if k > 1:
            q = q + p[1 - k]
    return p[0] + m + q


def tables(col_owner):
    owners = jnp.arange(NX, dtype=I32)
    onehot = (col_owner[:, None] == owners[None, :]).astype(I32)
    rank = jnp.sum((jnp.cumsum(onehot, axis=0) - onehot) * onehot, axis=1)
    slots = jnp.arange(CAPC, dtype=I32)
    hit = (col_owner[None, None, :] == owners[:, None, None]) & (rank[None, None, :] == slots[None, :, None])
    owned = jnp.sum(hit.astype(I32) * jnp.arange(DB, dtype=I32)[None, None, :], axis=2)
    return owned, jnp.any(hit, axis=2).astype(I32)


def on_device(hidden, out_grad, act_rows, col_owner):
    b = lax.axis_index("blk")
    d = lax.axis_index("dp")
    z, core = d // 2, d % 2

    h_l = x_right(hidden)
    h_r = x_left(hidden)
    g_all = lax.all_gather(out_grad, "team", axis=0, tiled=False)

    owned, alive = tables(col_owner)
    zd = (z + jnp.array(OFFS, I32)) % NZ

    order = jnp.concatenate([3 * zd + 1, 3 * zd + 2 * core, 3 * zd + 2 * (1 - core)])
    dest = (b + jnp.array((1, -1, 2, 0), I32)) % NX
    cols = jnp.take(jnp.take(owned, dest, axis=0), order, axis=1)
    live = jnp.take(jnp.take(alive, dest, axis=0), order, axis=1)
    mine = cols[3]
    rows = jnp.take(act_rows[0], mine[:16], axis=0)
    rows_a = lax.dynamic_slice_in_dim(rows[:8], 6 * core, 6, axis=1).reshape(-1)
    rows_b = rows[8:, :6].reshape(-1)
    rows_c = rows[8:, 6:].reshape(-1)

    h_o = other_core(hidden)
    r0, l0, o0, r1, l1, o1 = pick(cols.reshape(-1), live.reshape(-1), g_all)

    def spread(r, l, o):
        r, l = x_right(r), x_left(l)
        f, e = x_right(r[128:]), x_left(l[128:])
        return jnp.concatenate([o, r[:128], l[:128], f, e], axis=0)

    g0 = spread(r0, l0, o0)
    g0o = other_core(g0)
    h_f = x_right(h_l[:64])
    h_e = x_left(h_r[64:])
    r1, l1, h_f, h_e = lax.optimization_barrier((r1, l1, h_f, h_e))
    h_lo, h_ro = other_core(h_l), other_core(h_r)
    h_fo, h_eo = other_core(h_f), other_core(h_e)
    hs = (hidden, h_l, h_r, h_f, h_e, h_o, h_lo, h_ro, h_fo, h_eo)
    pa = gemm(6, rows_a, hs, (g0, g0o))
    g1 = spread(r1, l1, o1)
    g1o = other_core(g1[:, 1024:])
    g1 = g1[:, :1024]
    pb = gemm(6, rows_b, hs, (g1, g1o))
    pc = gemm(6, rows_c, hs, (g1, g1o))
    a = ring_sum(pa, 4, 3)
    bsum = ring_sum(pb, 3, 4)
    c = ring_sum(pc, 4, 3)
    first = jnp.concatenate([bsum, c, a])
    second = jnp.concatenate([a, bsum, c])
    gradients = jnp.where(core == 0, first, second)
    scores = jnp.sqrt(jnp.mean(gradients * gradients, axis=(1, 2)) + EPS)
    return gradients[None, None], scores[None, None]


def solution(mesh):
    in_specs = (P(("blk", "dp"), "team"), P(("blk", "dp"), "team"), P("team", None, None), P())
    out_specs = (P("team", "blk", "dp", None, None), P("team", "blk", "dp"))
    return jax.shard_map(on_device, mesh=mesh, in_specs=in_specs, out_specs=out_specs, check_vma=False)
```

```python
import functools

import jax
import jax.numpy as jnp
from jax import lax
from jax.experimental import pallas as pl
from jax.experimental.pallas import tpu as pltpu
from jax.sharding import PartitionSpec as P

BS = 128
NX, NZ = 4, 8
CAPC, KC, DB = 24, 12, 64
EPS = 1e-06
F32, BF16, I32 = jnp.float32, jnp.bfloat16, jnp.int32
OFFS = (4, 3, 2, 1, 0, -1, -2, -3)
VMEM = pl.BlockSpec(memory_space=pltpu.VMEM)
SMEM = pl.BlockSpec(memory_space=pltpu.SMEM)
ANY = pl.BlockSpec(memory_space=pl.ANY)


def perm(x, axis, n, step):
    return lax.ppermute(x, axis, [(i, (i + step) % n) for i in range(n)])


def x_right(v):
    return perm(v, "blk", NX, 1)


def x_left(v):
    return perm(v, "blk", NX, -1)


def z_right(v):
    return perm(v, "dp", 2 * NZ, 2)


def z_left(v):
    return perm(v, "dp", 2 * NZ, -2)


def other_core(v):
    return lax.ppermute(v, "dp", [(i, i ^ 1) for i in range(2 * NZ)])


def plan_kernel(meta, owner, act, cols, rows, owned, count):
    b, t, z, core = meta[0], meta[1], meta[2], meta[3]
    for i in range(NX * CAPC):
        owned[i] = -1
    for i in range(NX):
        count[i] = 0

    def note(c, _):
        o = owner[c]
        j = count[o]

        @pl.when(j < CAPC)
        def _():
            owned[o * CAPC + j] = c

        count[o] = j + 1
        return 0

    lax.fori_loop(0, DB, note, 0)
    side = (1, 2 * core, 2 * (1 - core))
    for e, step in enumerate((1, NX - 1, 2, 0)):
        o = lax.rem(b + step, NX)
        for s in range(CAPC):
            zd = lax.rem(z + OFFS[s % 8] + NZ, NZ)
            c = owned[o * CAPC + 3 * zd + side[s // 8]]
            cols[e * CAPC + s] = jnp.where(c < 0, -1, lax.rem(c - 16 * t + DB, DB))
            if e == 3 and s < 16:
                at = jnp.maximum(c, 0) * KC
                for i in range(6):
                    if s < 8:
                        rows[s * 6 + i] = act[at + 6 * core + i]
                    else:
                        rows[48 + (s - 8) * 6 + i] = act[at + i]
                        rows[96 + (s - 8) * 6 + i] = act[at + 6 + i]


def plan(meta, owner, act):
    return pl.pallas_call(
        plan_kernel,
        out_shape=[jax.ShapeDtypeStruct((NX * CAPC,), I32), jax.ShapeDtypeStruct((144,), I32)],
        in_specs=[SMEM] * 3,
        out_specs=[SMEM] * 2,
        scratch_shapes=[pltpu.SMEM((NX * CAPC,), I32), pltpu.SMEM((NX,), I32)],
        compiler_params=pltpu.CompilerParams(vmem_limit_bytes=4 * 2**20),
        cost_estimate=pl.CostEstimate(flops=0, bytes_accessed=4096, transcendentals=0),
        name="plan",
    )(meta, owner, act)


def pick_kernel(cols, g, gu, gd, gf, ge, r0, l0, o0, r1, l1, rf, lf, o1, gv, sems):
    half = 64
    copies = [
        pltpu.make_async_copy(src, dst, sems.at[i])
        for i, (src, dst) in enumerate(
            [(g, gv.at[0]), (gu, gv.at[1]), (gf, gv.at[2, 0:64]), (ge, gv.at[2, 64:128]), (gd, gv.at[3])]
        )
    ]
    for c in copies:
        c.start()
    for c in copies:
        c.wait()

    def put(e, s, ref, lane, row, lo, hi):
        a = cols[e * CAPC + s]
        c = jnp.maximum(a, 0)
        v = gv[c // 16, lo:hi, pl.ds(pl.multiple_of((c % 16) * BS, BS), BS)]
        ref[row : row + hi - lo, lane * BS : (lane + 1) * BS] = jnp.where(a >= 0, v, jnp.zeros_like(v))

    for s in range(CAPC):
        if s < 8:
            put(0, s, r0, s, 0, 0, 128)
            put(2, s, r0, s, 128, 0, half)
            put(1, s, l0, s, 0, 0, 128)
            put(2, s, l0, s, 128, half, 128)
            put(3, s, o0, s, 0, 0, 128)
        else:
            put(0, s, r1, s - 8, 0, 0, 128)
            put(2, s, rf, s - 8, 0, 0, half)
            put(1, s, l1, s - 8, 0, 0, 128)
            put(2, s, lf, s - 8, 0, half, 128)
            put(3, s, o1, s - 8, 0, 0, 128)


def pick(cols, gs):
    shapes = [(192, 1024), (192, 1024), (128, 1024), (128, 2048), (128, 2048), (64, 2048), (64, 2048), (128, 2048)]
    return pl.pallas_call(
        pick_kernel,
        out_shape=[jax.ShapeDtypeStruct(s, BF16) for s in shapes],
        in_specs=[SMEM] + [ANY] * 5,
        out_specs=[VMEM] * len(shapes),
        scratch_shapes=[pltpu.VMEM((4, 128, 2048), BF16), pltpu.SemaphoreType.DMA((5,))],
        compiler_params=pltpu.CompilerParams(vmem_limit_bytes=14 * 2**20),
        cost_estimate=pl.CostEstimate(flops=0, bytes_accessed=6 * 2**20, transcendentals=0),
        name="pick_columns",
    )(cols, *gs)


def encode(ref, i, v):
    top = jnp.max(jnp.abs(v), axis=0, keepdims=True)
    q = jnp.ceil(jnp.log2(jnp.maximum(top, 1e-30)) * 8.0 + 0.01)
    code = jnp.round(v * (jnp.exp2(q * -0.125) * 32766.0))
    ref[i * BS : (i + 1) * BS, :] = code.astype(I32).astype(jnp.int16)
    return q


def put_scales(ref, n, qs):
    pad = jnp.zeros((16 - n, BS), F32)
    ref[n * BS : n * BS + 16, :] = jnp.concatenate(list(qs) + [pad], axis=0).astype(I32).astype(jnp.int16)


def scales(ref, n):
    q = ref[n * BS : n * BS + 16, :].astype(I32).astype(F32)
    return jnp.exp2(q * 0.125) * (1.0 / 32766.0)


def decode(ref, i, scale):
    return ref[i * BS : (i + 1) * BS, :].astype(I32).astype(F32) * scale[i : i + 1, :]


def message(n):
    return jax.ShapeDtypeStruct((n * BS + 16, BS), jnp.int16)


def move_kernel(moves, n, *refs):
    for i, ci, rows, lanes, o, ro, co in moves:
        refs[n + o][ro : ro + rows, co : co + lanes] = refs[i][0:rows, ci : ci + lanes]


def move(ins, shapes, moves, name):
    return pl.pallas_call(
        functools.partial(move_kernel, moves, len(ins)),
        out_shape=[jax.ShapeDtypeStruct(s, BF16) for s in shapes],
        grid=(1,),
        in_specs=[pl.BlockSpec((r, v.shape[1]), functools.partial(lambda j, i: (j, 0), j)) for v, r, j in ins],
        out_specs=[pl.BlockSpec(s, lambda i: (0, 0)) for s in shapes],
        compiler_params=pltpu.CompilerParams(vmem_limit_bytes=14 * 2**20),
        cost_estimate=pl.CostEstimate(flops=0, bytes_accessed=sum(4 * a * b for a, b in shapes), transcendentals=0),
        name=name,
    )(*[v for v, _, _ in ins])


def turn_kernel(*refs):
    ins, out = refs[:-1], refs[-1]
    for i, v in enumerate(ins):
        for c in range(out.shape[0] // BS):
            out[c * BS : (c + 1) * BS, i * BS : (i + 1) * BS] = v[:, c * BS : (c + 1) * BS].T


def turn(*hs):
    features, chunk = hs[0].shape[1], 896
    tokens = BS * len(hs)
    return pl.pallas_call(
        turn_kernel,
        out_shape=jax.ShapeDtypeStruct((features, tokens), BF16),
        grid=(features // chunk,),
        in_specs=[pl.BlockSpec((BS, chunk), lambda i: (0, i)) for h in hs],
        out_specs=pl.BlockSpec((chunk, tokens), lambda i: (i, 0)),
        compiler_params=pltpu.CompilerParams(vmem_limit_bytes=24 * 2**20),
        cost_estimate=pl.CostEstimate(flops=0, bytes_accessed=4 * tokens * features, transcendentals=0),
        name="turn",
    )(*hs)


def turn_far_kernel(p, q, po, qo, out, g):
    features = out.shape[0]
    for i, (a, b) in enumerate(((p, q), (po, qo))):
        for c in range(features // BS):
            at = slice(c * BS, (c + 1) * BS)
            v = jnp.concatenate([a[:, at], b[:, at]], axis=0)
            out[at, i * BS : (i + 1) * BS] = v.T
        g[i * BS : i * BS + 64] = a[:, features:]
        g[i * BS + 64 : (i + 1) * BS] = b[:, features:]


def turn_far(p, q, po, qo, features):
    return pl.pallas_call(
        turn_far_kernel,
        out_shape=[
            jax.ShapeDtypeStruct((features, 2 * BS), BF16),
            jax.ShapeDtypeStruct((2 * BS, p.shape[1] - features), BF16),
        ],
        in_specs=[VMEM] * 4,
        out_specs=[VMEM] * 2,
        compiler_params=pltpu.CompilerParams(vmem_limit_bytes=24 * 2**20),
        cost_estimate=pl.CostEstimate(flops=0, bytes_accessed=8 * 2**20, transcendentals=0),
        name="turn_far",
    )(p, q, po, qo)


def gemm_kernel(n, sent, base, pieces, rows, near, far, *refs):
    gs, outs = refs[: -len(OFFS)], refs[-len(OFFS) :]
    for k in range(len(OFFS)):
        at = slice(k * BS, (k + 1) * BS)
        b = jnp.concatenate([gs[i][lo:hi, at] for i, lo, hi in pieces], axis=0)
        a = []
        for i in range(n):
            r = pl.ds(pl.multiple_of(rows[base + k * n + i] * BS, BS), BS)
            a.append(jnp.concatenate([near[r, :], far[r, :]], axis=1))
        v = jnp.dot(jnp.concatenate(a, axis=0), b, preferred_element_type=F32)
        if k in sent:
            put_scales(outs[k], n, [encode(outs[k], i, v[i * BS : (i + 1) * BS]) for i in range(n)])
        else:
            for i in range(n):
                outs[k][i] = v[i * BS : (i + 1) * BS]


def gemm(n, base, rows, near, far, gs, pieces, right):
    sent = (0, 7) if right == 4 else (1, 0)
    outs = [message(n) if k in sent else jax.ShapeDtypeStruct((n, BS, BS), F32) for k in range(len(OFFS))]
    return pl.pallas_call(
        functools.partial(gemm_kernel, n, sent, base, pieces),
        out_shape=outs,
        in_specs=[SMEM] + [VMEM] * (2 + len(gs)),
        out_specs=[VMEM] * len(OFFS),
        compiler_params=pltpu.CompilerParams(vmem_limit_bytes=24 * 2**20),
        cost_estimate=pl.CostEstimate(
            flops=2 * len(OFFS) * n * 1024 * BS * BS, bytes_accessed=16 * 2**20, transcendentals=0
        ),
        name="block_products",
    )(rows, near, far, *gs)


def hop_kernel(n, m, p, o):
    scale = scales(m, n)
    qs = [encode(o, i, p[i] + decode(m, i, scale)) for i in range(n)]
    put_scales(o, n, qs)


def hop(m, p):
    n = p.shape[0]
    return pl.pallas_call(
        functools.partial(hop_kernel, n),
        out_shape=message(n),
        in_specs=[VMEM, VMEM],
        out_specs=VMEM,
        compiler_params=pltpu.CompilerParams(vmem_limit_bytes=6 * 2**20),
        cost_estimate=pl.CostEstimate(flops=10 * n * BS * BS, bytes_accessed=8 * n * BS * BS, transcendentals=0),
        name="add_and_send",
    )(m, p)


def ring_start(parts, right, left):
    p = dict(zip(OFFS, parts))
    p[-4] = p[4]
    return z_right(p[right]), z_left(p[-left])


def ring_sum(parts, m, q, right, left):
    p = dict(zip(OFFS, parts))
    for k in range(max(right, left) - 1, 0, -1):
        if k < right:
            m = z_right(hop(m, p[k]))
        if k < left:
            q = z_left(hop(q, p[-k]))
    return p[0], m, q


def finish_kernel(n, at, *refs):
    ins, out, ss = refs[:9], refs[9], refs[10]
    for j in range(3):
        p, m, q = ins[3 * j : 3 * j + 3]
        sm, sq = scales(m, n), scales(q, n)
        for i in range(n):
            v = p[i] + decode(m, i, sm) + decode(q, i, sq)
            out[at[j] + i] = v
            ss[pl.ds(at[j] + i, 1), :] = jnp.sum(v * v, axis=0, keepdims=True)


def finish(at, groups):
    n = groups[0][0].shape[0]
    flat = [v for g in groups for v in g]
    return pl.pallas_call(
        functools.partial(finish_kernel, n),
        out_shape=[jax.ShapeDtypeStruct((3 * n, BS, BS), F32), jax.ShapeDtypeStruct((3 * n, BS), F32)],
        in_specs=[SMEM] + [VMEM] * 9,
        out_specs=[VMEM, VMEM],
        compiler_params=pltpu.CompilerParams(vmem_limit_bytes=12 * 2**20),
        cost_estimate=pl.CostEstimate(flops=30 * n * BS * BS, bytes_accessed=36 * n * BS * BS, transcendentals=0),
        name="finish",
    )(at, *flat)


def on_device(hidden, out_grad, act_rows, col_owner):
    b = lax.axis_index("blk")
    t = lax.axis_index("team")
    d = lax.axis_index("dp")
    z, core = d // 2, d % 2

    features = hidden.shape[1]
    g_d = perm(out_grad, "team", NX, 1)
    g_u = perm(out_grad, "team", NX, -1)
    h_l, h_r = x_right(hidden), x_left(hidden)
    h_o = other_core(hidden)
    g_f = perm(g_d[:64], "team", NX, 1)
    g_e = perm(g_u[64:], "team", NX, -1)
    meta = jnp.stack([b, t, z, core]).astype(I32)
    cols, rows = plan(meta, col_owner, act_rows.reshape(-1))
    cols, h_o = lax.optimization_barrier((cols, h_o))
    r0, l0, o0, r1, l1, rf, lf, o1 = pick(cols, (out_grad, g_u, g_d, g_f, g_e))
    r0, l0 = x_right(r0), x_left(l0)
    h_l, h_r, r0, l0 = lax.optimization_barrier((h_l, h_r, r0, l0))
    p, q = move(
        ((h_l, 64, 0), (h_r, 64, 1), (r0, 64, 2), (l0, 64, 2)),
        [(64, features + 1024)] * 2,
        (
            (0, 0, 64, features, 0, 0, 0),
            (2, 0, 64, 1024, 0, 0, features),
            (1, 0, 64, features, 1, 0, 0),
            (3, 0, 64, 1024, 1, 0, features),
        ),
        "pack_far",
    )
    p, q = x_right(p), x_left(q)
    (g0,) = move(
        ((o0, 128, 0), (r0, 128, 0), (l0, 128, 0)),
        [(384, 1024)],
        tuple((i, 0, 128, 1024, 0, 128 * i, 0) for i in range(3)),
        "join_near",
    )
    h_lo, h_ro, g0o = other_core(h_l), other_core(h_r), other_core(g0)
    near = turn(hidden, h_l, h_r, h_o, h_lo, h_ro)
    p, q, r1, l1, rf, lf, near, g0o = lax.optimization_barrier((p, q, r1, l1, rf, lf, near, g0o))
    rf, lf = x_right(rf), x_left(lf)
    r1, l1 = x_right(r1), x_left(l1)
    po, qo = other_core(p), other_core(q)
    po, qo, rf, lf = lax.optimization_barrier((po, qo, rf, lf))
    rf, lf = x_right(rf), x_left(lf)
    far, gf = turn_far(p, q, po, qo, features)
    pa = gemm(6, 0, rows, near, far, (g0, g0o, gf), ((0, 0, 384), (1, 0, 384), (2, 0, 256)), 4)
    ma, qa = ring_start(pa, 4, 3)
    r1, l1, rf, lf, ma, qa = lax.optimization_barrier((r1, l1, rf, lf, ma, qa))
    g1, g1o = move(
        ((o1, 128, 0), (r1, 128, 0), (l1, 128, 0), (rf, 64, 0), (lf, 64, 0)),
        [(512, 1024)] * 2,
        tuple(
            (i, 1024 * j, n, 1024, j, at, 0)
            for j in range(2)
            for i, n, at in ((0, 128, 0), (1, 128, 128), (2, 128, 256), (3, 64, 384), (4, 64, 448))
        ),
        "join",
    )
    g1o = other_core(g1o)
    pieces = ((0, 0, 384), (1, 0, 384), (0, 384, 512), (1, 384, 512))
    pb = gemm(6, 48, rows, near, far, (g1, g1o), pieces, 3)
    pc = gemm(6, 96, rows, near, far, (g1, g1o), pieces, 4)
    mb, qb = ring_start(pb, 3, 4)
    mc, qc = ring_start(pc, 4, 3)
    groups = [ring_sum(pa, ma, qa, 4, 3), ring_sum(pb, mb, qb, 3, 4), ring_sum(pc, mc, qc, 4, 3)]
    at = jnp.where(core == 0, jnp.array((12, 0, 6), I32), jnp.array((0, 6, 12), I32))
    gradients, squares = finish(at, groups)
    scores = jnp.sqrt(jnp.sum(squares, axis=1) * (1.0 / (BS * BS)) + EPS)
    return gradients[None, None], scores[None, None]


def solution(mesh):
    in_specs = (P(("blk", "dp"), "team"), P(("blk", "dp"), "team"), P("team", None, None), P())
    out_specs = (P("team", "blk", "dp", None, None), P("team", "blk", "dp"))
    return jax.shard_map(on_device, mesh=mesh, in_specs=in_specs, out_specs=out_specs, check_vma=False)
```

```python
import functools

import jax
import jax.numpy as jnp
from jax import lax
from jax.experimental import pallas as pl
from jax.experimental.pallas import tpu as pltpu
from jax.sharding import PartitionSpec as P

BS = 128
NX, NZ = 4, 8
CAPC, KC, DB = 24, 12, 64
EPS = 1e-06
F32, BF16, I32 = jnp.float32, jnp.bfloat16, jnp.int32
OFFS = (4, 3, 2, 1, 0, -1, -2, -3)
VMEM = pl.BlockSpec(memory_space=pltpu.VMEM)
SMEM = pl.BlockSpec(memory_space=pltpu.SMEM)
ANY = pl.BlockSpec(memory_space=pl.ANY)


def perm(x, axis, n, step):
    return lax.ppermute(x, axis, [(i, (i + step) % n) for i in range(n)])


def x_right(v):
    return perm(v, "blk", NX, 1)


def x_left(v):
    return perm(v, "blk", NX, -1)


def z_right(v):
    return perm(v, "dp", 2 * NZ, 2)


def z_left(v):
    return perm(v, "dp", 2 * NZ, -2)


def other_core(v):
    return lax.ppermute(v, "dp", [(i, i ^ 1) for i in range(2 * NZ)])


def plan_kernel(meta, owner, act, cols, rows, owned, count):
    b, t, z, core = meta[0], meta[1], meta[2], meta[3]
    for i in range(NX * CAPC):
        owned[i] = -1
    for i in range(NX):
        count[i] = 0

    def note(c, _):
        o = owner[c]
        j = count[o]

        @pl.when(j < CAPC)
        def _():
            owned[o * CAPC + j] = c

        count[o] = j + 1
        return 0

    lax.fori_loop(0, DB, note, 0)
    side = (1, 2 * core, 2 * (1 - core))
    for e, step in enumerate((1, NX - 1, 2, 0)):
        o = lax.rem(b + step, NX)
        for s in range(CAPC):
            zd = lax.rem(z + OFFS[s % 8] + NZ, NZ)
            c = owned[o * CAPC + 3 * zd + side[s // 8]]
            cols[e * CAPC + s] = jnp.where(c < 0, -1, lax.rem(c - 16 * t + DB, DB))
            if e == 3 and s < 16:
                at = jnp.maximum(c, 0) * KC
                for i in range(6):
                    if s < 8:
                        rows[s * 6 + i] = act[at + 6 * core + i]
                    else:
                        rows[48 + (s - 8) * 6 + i] = act[at + i]
                        rows[96 + (s - 8) * 6 + i] = act[at + 6 + i]


def plan(meta, owner, act):
    return pl.pallas_call(
        plan_kernel,
        out_shape=[jax.ShapeDtypeStruct((NX * CAPC,), I32), jax.ShapeDtypeStruct((144,), I32)],
        in_specs=[SMEM] * 3,
        out_specs=[SMEM] * 2,
        scratch_shapes=[pltpu.SMEM((NX * CAPC,), I32), pltpu.SMEM((NX,), I32)],
        compiler_params=pltpu.CompilerParams(vmem_limit_bytes=4 * 2**20),
        cost_estimate=pl.CostEstimate(flops=0, bytes_accessed=4096, transcendentals=0),
        name="plan",
    )(meta, owner, act)


def pick_kernel(cols, g, gu, gd, gf, ge, r0, l0, o0, r1, l1, rf, lf, o1, gv, sems):
    half = 64
    copies = [
        pltpu.make_async_copy(src, dst, sems.at[i])
        for i, (src, dst) in enumerate(
            [(g, gv.at[0]), (gu, gv.at[1]), (gf, gv.at[2, 0:64]), (ge, gv.at[2, 64:128]), (gd, gv.at[3])]
        )
    ]
    for c in copies:
        c.start()
    for c in copies:
        c.wait()

    def put(e, s, ref, lane, row, lo, hi):
        a = cols[e * CAPC + s]
        c = jnp.maximum(a, 0)
        v = gv[c // 16, lo:hi, pl.ds(pl.multiple_of((c % 16) * BS, BS), BS)]
        ref[row : row + hi - lo, lane * BS : (lane + 1) * BS] = jnp.where(a >= 0, v, jnp.zeros_like(v))

    for s in range(CAPC):
        if s < 8:
            put(0, s, r0, s, 0, 0, 128)
            put(2, s, r0, s, 128, 0, half)
            put(1, s, l0, s, 0, 0, 128)
            put(2, s, l0, s, 128, half, 128)
            put(3, s, o0, s, 0, 0, 128)
        else:
            put(0, s, r1, s - 8, 0, 0, 128)
            put(2, s, rf, s - 8, 0, 0, half)
            put(1, s, l1, s - 8, 0, 0, 128)
            put(2, s, lf, s - 8, 0, half, 128)
            put(3, s, o1, s - 8, 0, 0, 128)


def pick(cols, gs):
    shapes = [(192, 1024), (192, 1024), (128, 1024), (128, 2048), (128, 2048), (64, 2048), (64, 2048), (128, 2048)]
    return pl.pallas_call(
        pick_kernel,
        out_shape=[jax.ShapeDtypeStruct(s, BF16) for s in shapes],
        in_specs=[SMEM] + [ANY] * 5,
        out_specs=[VMEM] * len(shapes),
        scratch_shapes=[pltpu.VMEM((4, 128, 2048), BF16), pltpu.SemaphoreType.DMA((5,))],
        compiler_params=pltpu.CompilerParams(vmem_limit_bytes=14 * 2**20),
        cost_estimate=pl.CostEstimate(flops=0, bytes_accessed=6 * 2**20, transcendentals=0),
        name="pick_columns",
    )(cols, *gs)


def encode(ref, i, v):
    top = jnp.max(jnp.abs(v), axis=0, keepdims=True)
    q = jnp.ceil(jnp.log2(jnp.maximum(top, 1e-30)) * 8.0 + 0.01)
    code = jnp.round(v * (jnp.exp2(q * -0.125) * 32766.0))
    ref[i * BS : (i + 1) * BS, :] = code.astype(I32).astype(jnp.int16)
    return q


def put_scales(ref, n, qs):
    pad = jnp.zeros((16 - n, BS), F32)
    ref[n * BS : n * BS + 16, :] = jnp.concatenate(list(qs) + [pad], axis=0).astype(I32).astype(jnp.int16)


def scales(ref, n):
    q = ref[n * BS : n * BS + 16, :].astype(I32).astype(F32)
    return jnp.exp2(q * 0.125) * (1.0 / 32766.0)


def decode(ref, i, scale):
    return ref[i * BS : (i + 1) * BS, :].astype(I32).astype(F32) * scale[i : i + 1, :]


def message(n):
    return jax.ShapeDtypeStruct((n * BS + 16, BS), jnp.int16)


def move_kernel(moves, n, *refs):
    for i, ci, rows, lanes, o, ro, co in moves:
        refs[n + o][ro : ro + rows, co : co + lanes] = refs[i][0:rows, ci : ci + lanes]


def move(ins, shapes, moves, name):
    return pl.pallas_call(
        functools.partial(move_kernel, moves, len(ins)),
        out_shape=[jax.ShapeDtypeStruct(s, BF16) for s in shapes],
        grid=(1,),
        in_specs=[pl.BlockSpec((r, v.shape[1]), functools.partial(lambda j, i: (j, 0), j)) for v, r, j in ins],
        out_specs=[pl.BlockSpec(s, lambda i: (0, 0)) for s in shapes],
        compiler_params=pltpu.CompilerParams(vmem_limit_bytes=14 * 2**20),
        cost_estimate=pl.CostEstimate(flops=0, bytes_accessed=sum(4 * a * b for a, b in shapes), transcendentals=0),
        name=name,
    )(*[v for v, _, _ in ins])


def turn_kernel(*refs):
    ins, out = refs[:-1], refs[-1]
    for i, v in enumerate(ins):
        for c in range(out.shape[0] // BS):
            out[c * BS : (c + 1) * BS, i * BS : (i + 1) * BS] = v[:, c * BS : (c + 1) * BS].T


def turn(*hs):
    features, chunk = hs[0].shape[1], 896
    tokens = BS * len(hs)
    return pl.pallas_call(
        turn_kernel,
        out_shape=jax.ShapeDtypeStruct((features, tokens), BF16),
        grid=(features // chunk,),
        in_specs=[pl.BlockSpec((BS, chunk), lambda i: (0, i)) for h in hs],
        out_specs=pl.BlockSpec((chunk, tokens), lambda i: (i, 0)),
        compiler_params=pltpu.CompilerParams(vmem_limit_bytes=24 * 2**20),
        cost_estimate=pl.CostEstimate(flops=0, bytes_accessed=4 * tokens * features, transcendentals=0),
        name="turn",
    )(*hs)


def turn_far_kernel(p, q, po, qo, out, g):
    features = out.shape[0]
    for i, (a, b) in enumerate(((p, q), (po, qo))):
        for c in range(features // BS):
            at = slice(c * BS, (c + 1) * BS)
            v = jnp.concatenate([a[:, at], b[:, at]], axis=0)
            out[at, i * BS : (i + 1) * BS] = v.T
        g[i * BS : i * BS + 64] = a[:, features:]
        g[i * BS + 64 : (i + 1) * BS] = b[:, features:]


def turn_far(p, q, po, qo, features):
    return pl.pallas_call(
        turn_far_kernel,
        out_shape=[
            jax.ShapeDtypeStruct((features, 2 * BS), BF16),
            jax.ShapeDtypeStruct((2 * BS, p.shape[1] - features), BF16),
        ],
        in_specs=[VMEM] * 4,
        out_specs=[VMEM] * 2,
        compiler_params=pltpu.CompilerParams(vmem_limit_bytes=24 * 2**20),
        cost_estimate=pl.CostEstimate(flops=0, bytes_accessed=8 * 2**20, transcendentals=0),
        name="turn_far",
    )(p, q, po, qo)


def gemm_kernel(n, groups, pieces, rows, near, far, *refs):
    ng = len(refs) - len(groups) * len(OFFS)
    gs, outs = refs[:ng], refs[ng:]
    for k in range(len(OFFS)):
        at = slice(k * BS, (k + 1) * BS)
        b = jnp.concatenate([gs[i][lo:hi, at] for i, lo, hi in pieces], axis=0)
        a = []
        for base, _ in groups:
            for i in range(n):
                r = pl.ds(pl.multiple_of(rows[base + k * n + i] * BS, BS), BS)
                a.append(jnp.concatenate([near[r, :], far[r, :]], axis=1))
        v = jnp.dot(jnp.concatenate(a, axis=0), b, preferred_element_type=F32)
        for j, (_, right) in enumerate(groups):
            out = outs[j * len(OFFS) + k]
            block = [v[(j * n + i) * BS : (j * n + i + 1) * BS] for i in range(n)]
            if k in SENT[right]:
                put_scales(out, n, [encode(out, i, block[i]) for i in range(n)])
            else:
                for i in range(n):
                    out[i] = block[i]


SENT = {4: (0, 7), 3: (1, 0)}


def gemm(n, groups, rows, near, far, gs, pieces):
    outs = []
    for _, right in groups:
        outs += [message(n) if k in SENT[right] else jax.ShapeDtypeStruct((n, BS, BS), F32) for k in range(len(OFFS))]
    out = pl.pallas_call(
        functools.partial(gemm_kernel, n, groups, pieces),
        out_shape=outs,
        in_specs=[SMEM] + [VMEM] * (2 + len(gs)),
        out_specs=[VMEM] * len(outs),
        compiler_params=pltpu.CompilerParams(vmem_limit_bytes=24 * 2**20),
        cost_estimate=pl.CostEstimate(
            flops=2 * len(outs) * n * 1024 * BS * BS, bytes_accessed=16 * 2**20, transcendentals=0
        ),
        name="block_products",
    )(rows, near, far, *gs)
    return [out[i : i + len(OFFS)] for i in range(0, len(outs), len(OFFS))]


def hop_kernel(n, m, p, o):
    scale = scales(m, n)
    qs = [encode(o, i, p[i] + decode(m, i, scale)) for i in range(n)]
    put_scales(o, n, qs)


def hop(m, p):
    n = p.shape[0]
    return pl.pallas_call(
        functools.partial(hop_kernel, n),
        out_shape=message(n),
        in_specs=[VMEM, VMEM],
        out_specs=VMEM,
        compiler_params=pltpu.CompilerParams(vmem_limit_bytes=6 * 2**20),
        cost_estimate=pl.CostEstimate(flops=10 * n * BS * BS, bytes_accessed=8 * n * BS * BS, transcendentals=0),
        name="add_and_send",
    )(m, p)


def ring_start(parts, right, left):
    p = dict(zip(OFFS, parts))
    p[-4] = p[4]
    return z_right(p[right]), z_left(p[-left])


def ring_sum(parts, m, q, right, left, done=1):
    p = dict(zip(OFFS, parts))
    for k in range(max(right, left) - 1, 0, -1):
        if k <= right - done:
            m = z_right(hop(m, p[k]))
        if k <= left - done:
            q = z_left(hop(q, p[-k]))
    return p[0], m, q


def finish_kernel(n, at, *refs):
    ins, out, ss = refs[:9], refs[9], refs[10]
    for j in range(3):
        p, m, q = ins[3 * j : 3 * j + 3]
        sm, sq = scales(m, n), scales(q, n)
        for i in range(n):
            v = p[i] + decode(m, i, sm) + decode(q, i, sq)
            out[at[j] + i] = v
            ss[pl.ds(at[j] + i, 1), :] = jnp.sum(v * v, axis=0, keepdims=True)


def finish(at, groups):
    n = groups[0][0].shape[0]
    flat = [v for g in groups for v in g]
    return pl.pallas_call(
        functools.partial(finish_kernel, n),
        out_shape=[jax.ShapeDtypeStruct((3 * n, BS, BS), F32), jax.ShapeDtypeStruct((3 * n, BS), F32)],
        in_specs=[SMEM] + [VMEM] * 9,
        out_specs=[VMEM, VMEM],
        compiler_params=pltpu.CompilerParams(vmem_limit_bytes=12 * 2**20),
        cost_estimate=pl.CostEstimate(flops=30 * n * BS * BS, bytes_accessed=36 * n * BS * BS, transcendentals=0),
        name="finish",
    )(at, *flat)


def on_device(hidden, out_grad, act_rows, col_owner):
    b = lax.axis_index("blk")
    t = lax.axis_index("team")
    d = lax.axis_index("dp")
    z, core = d // 2, d % 2

    features = hidden.shape[1]
    g_d = perm(out_grad, "team", NX, 1)
    g_u = perm(out_grad, "team", NX, -1)
    h_l, h_r = x_right(hidden), x_left(hidden)
    h_o = other_core(hidden)
    g_f = perm(g_d[:64], "team", NX, 1)
    g_e = perm(g_u[64:], "team", NX, -1)
    meta = jnp.stack([b, t, z, core]).astype(I32)
    cols, rows = plan(meta, col_owner, act_rows.reshape(-1))
    cols, h_o = lax.optimization_barrier((cols, h_o))
    r0, l0, o0, r1, l1, rf, lf, o1 = pick(cols, (out_grad, g_u, g_d, g_f, g_e))
    r0, l0 = x_right(r0), x_left(l0)
    h_l, h_r, rf, lf = lax.optimization_barrier((h_l, h_r, rf, lf))
    rf, lf = x_right(rf), x_left(lf)
    h_l, h_r, r0, l0, rf, lf = lax.optimization_barrier((h_l, h_r, r0, l0, rf, lf))
    p, q = move(
        ((h_l, 64, 0), (h_r, 64, 1), (r0, 64, 2), (l0, 64, 2)),
        [(64, features + 1024)] * 2,
        (
            (0, 0, 64, features, 0, 0, 0),
            (2, 0, 64, 1024, 0, 0, features),
            (1, 0, 64, features, 1, 0, 0),
            (3, 0, 64, 1024, 1, 0, features),
        ),
        "pack_far",
    )
    p, q = x_right(p), x_left(q)
    (g0,) = move(
        ((o0, 128, 0), (r0, 128, 0), (l0, 128, 0)),
        [(384, 1024)],
        tuple((i, 0, 128, 1024, 0, 128 * i, 0) for i in range(3)),
        "join_near",
    )
    h_lo, h_ro, g0o = other_core(h_l), other_core(h_r), other_core(g0)
    near = turn(hidden, h_l, h_r, h_o, h_lo, h_ro)
    r1, l1 = move(
        ((r1, 128, 0), (l1, 128, 0), (rf, 64, 0), (lf, 64, 0)),
        [(192, 2048)] * 2,
        ((0, 0, 128, 2048, 0, 0, 0), (2, 0, 64, 2048, 0, 128, 0), (1, 0, 128, 2048, 1, 0, 0), (3, 0, 64, 2048, 1, 128, 0)),
        "pack",
    )
    p, q, r1, l1, near, g0o = lax.optimization_barrier((p, q, r1, l1, near, g0o))
    po, qo = other_core(p), other_core(q)
    r1, l1 = x_right(r1), x_left(l1)
    far, gf = turn_far(p, q, po, qo, features)
    (pa,) = gemm(6, ((0, 4),), rows, near, far, (g0, g0o, gf), ((0, 0, 384), (1, 0, 384), (2, 0, 256)))
    ma, qa = ring_start(pa, 4, 3)
    r1, l1, ma, qa = lax.optimization_barrier((r1, l1, ma, qa))
    ma, qa = z_right(hop(ma, pa[1])), z_left(hop(qa, pa[6]))
    g1, g1o = move(
        ((o1, 128, 0), (r1, 128, 0), (l1, 128, 0), (r1, 64, 2), (l1, 64, 2)),
        [(512, 1024)] * 2,
        tuple(
            (i, 1024 * j, n, 1024, j, at, 0)
            for j in range(2)
            for i, n, at in ((0, 128, 0), (1, 128, 128), (2, 128, 256), (3, 64, 384), (4, 64, 448))
        ),
        "join",
    )
    g1o = other_core(g1o)
    pieces = ((0, 0, 384), (1, 0, 384), (0, 384, 512), (1, 384, 512))
    pb, pc = gemm(6, ((48, 3), (96, 4)), rows, near, far, (g1, g1o), pieces)
    mb, qb, mc, qc, ma, qa = lax.optimization_barrier((pb[1], pb[0], pc[0], pc[7], ma, qa))
    mb, qb, mc, qc = z_right(mb), z_left(qb), z_right(mc), z_left(qc)
    groups = [ring_sum(pa, ma, qa, 4, 3, 2), ring_sum(pb, mb, qb, 3, 4), ring_sum(pc, mc, qc, 4, 3)]
    at = jnp.where(core == 0, jnp.array((12, 0, 6), I32), jnp.array((0, 6, 12), I32))
    gradients, squares = finish(at, groups)
    scores = jnp.sqrt(jnp.sum(squares, axis=1) * (1.0 / (BS * BS)) + EPS)
    return gradients[None, None], scores[None, None]


def solution(mesh):
    in_specs = (P(("blk", "dp"), "team"), P(("blk", "dp"), "team"), P("team", None, None), P())
    out_specs = (P("team", "blk", "dp", None, None), P("team", "blk", "dp"))
    return jax.shard_map(on_device, mesh=mesh, in_specs=in_specs, out_specs=out_specs, check_vma=False)
```

```python
import functools

import jax
import jax.numpy as jnp
from jax import lax
from jax.experimental import pallas as pl
from jax.experimental.pallas import tpu as pltpu
from jax.sharding import PartitionSpec as P

BS = 128
NX, NZ = 4, 8
CAPC, KC, DB = 24, 12, 64
EPS = 1e-06
F32, BF16, I32 = jnp.float32, jnp.bfloat16, jnp.int32
OFFS = (4, 3, 2, 1, 0, -1, -2, -3)
VMEM = pl.BlockSpec(memory_space=pltpu.VMEM)
SMEM = pl.BlockSpec(memory_space=pltpu.SMEM)
ANY = pl.BlockSpec(memory_space=pl.ANY)


def perm(x, axis, n, step):
    return lax.ppermute(x, axis, [(i, (i + step) % n) for i in range(n)])


def x_right(v):
    return perm(v, "blk", NX, 1)


def x_left(v):
    return perm(v, "blk", NX, -1)


def z_right(v):
    return perm(v, "dp", 2 * NZ, 2)


def z_left(v):
    return perm(v, "dp", 2 * NZ, -2)


def other_core(v):
    return lax.ppermute(v, "dp", [(i, i ^ 1) for i in range(2 * NZ)])


def plan_kernel(meta, owner, act, cols, rows, owned, count):
    b, t, z, core = meta[0], meta[1], meta[2], meta[3]
    for i in range(NX * CAPC):
        owned[i] = -1
    for i in range(NX):
        count[i] = 0

    def note(c, _):
        o = owner[c]
        j = count[o]

        @pl.when(j < CAPC)
        def _():
            owned[o * CAPC + j] = c

        count[o] = j + 1
        return 0

    lax.fori_loop(0, DB, note, 0)
    side = (1, 2 * core, 2 * (1 - core))
    for e, step in enumerate((1, NX - 1, 2, 0)):
        o = lax.rem(b + step, NX)
        for s in range(CAPC):
            zd = lax.rem(z + OFFS[s % 8] + NZ, NZ)
            c = owned[o * CAPC + 3 * zd + side[s // 8]]
            cols[e * CAPC + s] = jnp.where(c < 0, -1, lax.rem(c - 16 * t + DB, DB))
            if e == 3 and s < 16:
                at = jnp.maximum(c, 0) * KC
                for i in range(6):
                    if s < 8:
                        rows[s * 6 + i] = act[at + 6 * core + i]
                    else:
                        rows[48 + (s - 8) * 6 + i] = act[at + i]
                        rows[96 + (s - 8) * 6 + i] = act[at + 6 + i]


def plan(meta, owner, act):
    return pl.pallas_call(
        plan_kernel,
        out_shape=[jax.ShapeDtypeStruct((NX * CAPC,), I32), jax.ShapeDtypeStruct((144,), I32)],
        in_specs=[SMEM] * 3,
        out_specs=[SMEM] * 2,
        scratch_shapes=[pltpu.SMEM((NX * CAPC,), I32), pltpu.SMEM((NX,), I32)],
        compiler_params=pltpu.CompilerParams(vmem_limit_bytes=4 * 2**20),
        cost_estimate=pl.CostEstimate(flops=0, bytes_accessed=4096, transcendentals=0),
        name="plan",
    )(meta, owner, act)


def pick_kernel(cols, g, gu, gd, gf, ge, r0, l0, o0, r1, l1, rf, lf, o1, gv, sems):
    half = 64
    copies = [
        pltpu.make_async_copy(src, dst, sems.at[i])
        for i, (src, dst) in enumerate(
            [(g, gv.at[0]), (gu, gv.at[1]), (gf, gv.at[2, 0:64]), (ge, gv.at[2, 64:128]), (gd, gv.at[3])]
        )
    ]
    for c in copies:
        c.start()
    for c in copies:
        c.wait()

    def put(e, s, ref, lane, row, lo, hi):
        a = cols[e * CAPC + s]
        c = jnp.maximum(a, 0)
        v = gv[c // 16, lo:hi, pl.ds(pl.multiple_of((c % 16) * BS, BS), BS)]
        ref[row : row + hi - lo, lane * BS : (lane + 1) * BS] = jnp.where(a >= 0, v, jnp.zeros_like(v))

    for s in range(CAPC):
        if s < 8:
            put(0, s, r0, s, 0, 0, 128)
            put(2, s, r0, s, 128, 0, half)
            put(1, s, l0, s, 0, 0, 128)
            put(2, s, l0, s, 128, half, 128)
            put(3, s, o0, s, 0, 0, 128)
        else:
            put(0, s, r1, s - 8, 0, 0, 128)
            put(2, s, rf, s - 8, 0, 0, half)
            put(1, s, l1, s - 8, 0, 0, 128)
            put(2, s, lf, s - 8, 0, half, 128)
            put(3, s, o1, s - 8, 0, 0, 128)


def pick(cols, gs):
    shapes = [(192, 1024), (192, 1024), (128, 1024), (128, 2048), (128, 2048), (64, 2048), (64, 2048), (128, 2048)]
    return pl.pallas_call(
        pick_kernel,
        out_shape=[jax.ShapeDtypeStruct(s, BF16) for s in shapes],
        in_specs=[SMEM] + [ANY] * 5,
        out_specs=[VMEM] * len(shapes),
        scratch_shapes=[pltpu.VMEM((4, 128, 2048), BF16), pltpu.SemaphoreType.DMA((5,))],
        compiler_params=pltpu.CompilerParams(vmem_limit_bytes=14 * 2**20),
        cost_estimate=pl.CostEstimate(flops=0, bytes_accessed=6 * 2**20, transcendentals=0),
        name="pick_columns",
    )(cols, *gs)


def encode(ref, i, v):
    top = jnp.max(jnp.abs(v), axis=0, keepdims=True)
    q = jnp.ceil(jnp.log2(jnp.maximum(top, 1e-30)) * 8.0 + 0.01)
    code = jnp.round(v * (jnp.exp2(q * -0.125) * 32766.0))
    ref[i * BS : (i + 1) * BS, :] = code.astype(I32).astype(jnp.int16)
    return q


def put_scales(ref, n, qs):
    pad = jnp.zeros((16 - n, BS), F32)
    ref[n * BS : n * BS + 16, :] = jnp.concatenate(list(qs) + [pad], axis=0).astype(I32).astype(jnp.int16)


def scales(ref, n):
    q = ref[n * BS : n * BS + 16, :].astype(I32).astype(F32)
    return jnp.exp2(q * 0.125) * (1.0 / 32766.0)


def decode(ref, i, scale):
    return ref[i * BS : (i + 1) * BS, :].astype(I32).astype(F32) * scale[i : i + 1, :]


def message(n):
    return jax.ShapeDtypeStruct((n * BS + 16, BS), jnp.int16)


def move_kernel(moves, n, *refs):
    for i, ci, rows, lanes, o, ro, co in moves:
        refs[n + o][ro : ro + rows, co : co + lanes] = refs[i][0:rows, ci : ci + lanes]


def move(ins, shapes, moves, name):
    return pl.pallas_call(
        functools.partial(move_kernel, moves, len(ins)),
        out_shape=[jax.ShapeDtypeStruct(s, BF16) for s in shapes],
        grid=(1,),
        in_specs=[pl.BlockSpec((r, v.shape[1]), functools.partial(lambda j, i: (j, 0), j)) for v, r, j in ins],
        out_specs=[pl.BlockSpec(s, lambda i: (0, 0)) for s in shapes],
        compiler_params=pltpu.CompilerParams(vmem_limit_bytes=14 * 2**20),
        cost_estimate=pl.CostEstimate(flops=0, bytes_accessed=sum(4 * a * b for a, b in shapes), transcendentals=0),
        name=name,
    )(*[v for v, _, _ in ins])


def turn_kernel(*refs):
    ins, out = refs[:-1], refs[-1]
    for i, v in enumerate(ins):
        for c in range(out.shape[0] // BS):
            out[c * BS : (c + 1) * BS, i * BS : (i + 1) * BS] = v[:, c * BS : (c + 1) * BS].T


def turn(*hs):
    features, chunk = hs[0].shape[1], 896
    tokens = BS * len(hs)
    return pl.pallas_call(
        turn_kernel,
        out_shape=jax.ShapeDtypeStruct((features, tokens), BF16),
        grid=(features // chunk,),
        in_specs=[pl.BlockSpec((BS, chunk), lambda i: (0, i)) for h in hs],
        out_specs=pl.BlockSpec((chunk, tokens), lambda i: (i, 0)),
        compiler_params=pltpu.CompilerParams(vmem_limit_bytes=24 * 2**20),
        cost_estimate=pl.CostEstimate(flops=0, bytes_accessed=4 * tokens * features, transcendentals=0),
        name="turn",
    )(*hs)


def turn_far_kernel(p, q, po, qo, out, g):
    features = out.shape[0]
    for i, (a, b) in enumerate(((p, q), (po, qo))):
        for c in range(features // BS):
            at = slice(c * BS, (c + 1) * BS)
            v = jnp.concatenate([a[:, at], b[:, at]], axis=0)
            out[at, i * BS : (i + 1) * BS] = v.T
        g[i * BS : i * BS + 64] = a[:, features:]
        g[i * BS + 64 : (i + 1) * BS] = b[:, features:]


def turn_far(p, q, po, qo, features):
    return pl.pallas_call(
        turn_far_kernel,
        out_shape=[
            jax.ShapeDtypeStruct((features, 2 * BS), BF16),
            jax.ShapeDtypeStruct((2 * BS, p.shape[1] - features), BF16),
        ],
        in_specs=[VMEM] * 4,
        out_specs=[VMEM] * 2,
        compiler_params=pltpu.CompilerParams(vmem_limit_bytes=24 * 2**20),
        cost_estimate=pl.CostEstimate(flops=0, bytes_accessed=8 * 2**20, transcendentals=0),
        name="turn_far",
    )(p, q, po, qo)


SENT = {4: (0, 7), 3: (1, 0)}


def gemm_kernel(n, jobs, pieces, rows, near, far, *refs):
    ng = len(refs) - len(jobs)
    gs, outs = refs[:ng], refs[ng:]
    for k in sorted({k for k, _, _ in jobs}):
        at = slice(k * BS, (k + 1) * BS)
        b = jnp.concatenate([gs[i][lo:hi, at] for i, lo, hi in pieces], axis=0)
        here = [(base, right, o) for (kk, base, right), o in zip(jobs, outs) if kk == k]
        a = []
        for base, _, _ in here:
            for i in range(n):
                r = pl.ds(pl.multiple_of(rows[base + k * n + i] * BS, BS), BS)
                a.append(jnp.concatenate([near[r, :], far[r, :]], axis=1))
        v = jnp.dot(jnp.concatenate(a, axis=0), b, preferred_element_type=F32)
        for j, (_, right, out) in enumerate(here):
            block = [v[(j * n + i) * BS : (j * n + i + 1) * BS] for i in range(n)]
            if k in SENT[right]:
                put_scales(out, n, [encode(out, i, block[i]) for i in range(n)])
            else:
                for i in range(n):
                    out[i] = block[i]


def gemm(n, jobs, rows, near, far, gs, pieces):
    outs = [message(n) if k in SENT[right] else jax.ShapeDtypeStruct((n, BS, BS), F32) for k, _, right in jobs]
    return pl.pallas_call(
        functools.partial(gemm_kernel, n, jobs, pieces),
        out_shape=outs,
        in_specs=[SMEM] + [VMEM] * (2 + len(gs)),
        out_specs=[VMEM] * len(outs),
        compiler_params=pltpu.CompilerParams(vmem_limit_bytes=24 * 2**20),
        cost_estimate=pl.CostEstimate(
            flops=2 * len(outs) * n * 1024 * BS * BS, bytes_accessed=16 * 2**20, transcendentals=0
        ),
        name="block_products",
    )(rows, near, far, *gs)


def hop_kernel(n, m, p, o):
    scale = scales(m, n)
    qs = [encode(o, i, p[i] + decode(m, i, scale)) for i in range(n)]
    put_scales(o, n, qs)


def hop(m, p):
    n = p.shape[0]
    return pl.pallas_call(
        functools.partial(hop_kernel, n),
        out_shape=message(n),
        in_specs=[VMEM, VMEM],
        out_specs=VMEM,
        compiler_params=pltpu.CompilerParams(vmem_limit_bytes=6 * 2**20),
        cost_estimate=pl.CostEstimate(flops=10 * n * BS * BS, bytes_accessed=8 * n * BS * BS, transcendentals=0),
        name="add_and_send",
    )(m, p)


def ring_start(parts, right, left):
    p = dict(zip(OFFS, parts))
    p[-4] = p[4]
    return z_right(p[right]), z_left(p[-left])


def ring_sum(parts, m, q, right, left, done=1):
    p = dict(zip(OFFS, parts))
    for k in range(max(right, left) - 1, 0, -1):
        if k <= right - done:
            m = z_right(hop(m, p[k]))
        if k <= left - done:
            q = z_left(hop(q, p[-k]))
    return p[0], m, q


def finish_kernel(n, at, *refs):
    ins, out, ss = refs[:9], refs[9], refs[10]
    for j in range(3):
        p, m, q = ins[3 * j : 3 * j + 3]
        sm, sq = scales(m, n), scales(q, n)
        for i in range(n):
            v = p[i] + decode(m, i, sm) + decode(q, i, sq)
            out[at[j] + i] = v
            ss[pl.ds(at[j] + i, 1), :] = jnp.sum(v * v, axis=0, keepdims=True)


def finish(at, groups):
    n = groups[0][0].shape[0]
    flat = [v for g in groups for v in g]
    return pl.pallas_call(
        functools.partial(finish_kernel, n),
        out_shape=[jax.ShapeDtypeStruct((3 * n, BS, BS), F32), jax.ShapeDtypeStruct((3 * n, BS), F32)],
        in_specs=[SMEM] + [VMEM] * 9,
        out_specs=[VMEM, VMEM],
        compiler_params=pltpu.CompilerParams(vmem_limit_bytes=12 * 2**20),
        cost_estimate=pl.CostEstimate(flops=30 * n * BS * BS, bytes_accessed=36 * n * BS * BS, transcendentals=0),
        name="finish",
    )(at, *flat)


def on_device(hidden, out_grad, act_rows, col_owner):
    b = lax.axis_index("blk")
    t = lax.axis_index("team")
    d = lax.axis_index("dp")
    z, core = d // 2, d % 2

    features = hidden.shape[1]
    g_d = perm(out_grad, "team", NX, 1)
    g_u = perm(out_grad, "team", NX, -1)
    h_l, h_r = x_right(hidden), x_left(hidden)
    h_o = other_core(hidden)
    g_f = perm(g_d[:64], "team", NX, 1)
    g_e = perm(g_u[64:], "team", NX, -1)
    meta = jnp.stack([b, t, z, core]).astype(I32)
    cols, rows = plan(meta, col_owner, act_rows.reshape(-1))
    cols, h_o = lax.optimization_barrier((cols, h_o))
    r0, l0, o0, r1, l1, rf, lf, o1 = pick(cols, (out_grad, g_u, g_d, g_f, g_e))
    r0, l0 = x_right(r0), x_left(l0)
    h_l, h_r, rf, lf = lax.optimization_barrier((h_l, h_r, rf, lf))
    rf, lf = x_right(rf), x_left(lf)
    h_l, h_r, r0, l0, rf, lf = lax.optimization_barrier((h_l, h_r, r0, l0, rf, lf))
    p, q = move(
        ((h_l, 64, 0), (h_r, 64, 1), (r0, 64, 2), (l0, 64, 2)),
        [(64, features + 1024)] * 2,
        (
            (0, 0, 64, features, 0, 0, 0),
            (2, 0, 64, 1024, 0, 0, features),
            (1, 0, 64, features, 1, 0, 0),
            (3, 0, 64, 1024, 1, 0, features),
        ),
        "pack_far",
    )
    p, q = x_right(p), x_left(q)
    (g0,) = move(
        ((o0, 128, 0), (r0, 128, 0), (l0, 128, 0)),
        [(384, 1024)],
        tuple((i, 0, 128, 1024, 0, 128 * i, 0) for i in range(3)),
        "join_near",
    )
    h_lo, h_ro, g0o = other_core(h_l), other_core(h_r), other_core(g0)
    near = turn(hidden, h_l, h_r, h_o, h_lo, h_ro)
    r1, l1 = move(
        ((r1, 128, 0), (l1, 128, 0), (rf, 64, 0), (lf, 64, 0)),
        [(192, 2048)] * 2,
        ((0, 0, 128, 2048, 0, 0, 0), (2, 0, 64, 2048, 0, 128, 0), (1, 0, 128, 2048, 1, 0, 0), (3, 0, 64, 2048, 1, 128, 0)),
        "pack",
    )
    p, q, r1, l1, near, g0o = lax.optimization_barrier((p, q, r1, l1, near, g0o))
    po, qo = other_core(p), other_core(q)
    r1, l1 = x_right(r1), x_left(l1)
    far, gf = turn_far(p, q, po, qo, features)
    pa = gemm(6, tuple((k, 0, 4) for k in range(8)), rows, near, far, (g0, g0o, gf), ((0, 0, 384), (1, 0, 384), (2, 0, 256)))
    ma, qa = ring_start(pa, 4, 3)
    r1, l1, ma, qa = lax.optimization_barrier((r1, l1, ma, qa))
    g1, g1o = move(
        ((o1, 128, 0), (r1, 128, 0), (l1, 128, 0), (r1, 64, 2), (l1, 64, 2)),
        [(512, 1024)] * 2,
        tuple(
            (i, 1024 * j, n, 1024, j, at, 0)
            for j in range(2)
            for i, n, at in ((0, 128, 0), (1, 128, 128), (2, 128, 256), (3, 64, 384), (4, 64, 448))
        ),
        "join",
    )
    g1o = other_core(g1o)
    pieces = ((0, 0, 384), (1, 0, 384), (0, 384, 512), (1, 384, 512))
    sent = ((1, 48, 3), (0, 48, 3), (0, 96, 4), (7, 96, 4))
    kept = tuple((k, base, right) for base, right in ((48, 3), (96, 4)) for k in range(8) if k not in SENT[right])
    ha, ja = hop(ma, pa[1]), hop(qa, pa[6])
    g1, ha, ja = lax.optimization_barrier((g1, ha, ja))
    ma, qa = z_right(ha), z_left(ja)
    mb, qb, mc, qc = gemm(6, sent, rows, near, far, (g1, g1o), pieces)
    mb, qb, mc = z_right(mb), z_left(qb), z_right(mc)
    qc = z_left(qc)
    rest = gemm(6, kept, rows, near, far, (g1, g1o), pieces)
    pb, pc = [None, None] + list(rest[:6]), [None] + list(rest[6:]) + [None]
    groups = [ring_sum(pa, ma, qa, 4, 3, 2), ring_sum(pb, mb, qb, 3, 4), ring_sum(pc, mc, qc, 4, 3)]
    at = jnp.where(core == 0, jnp.array((12, 0, 6), I32), jnp.array((0, 6, 12), I32))
    gradients, squares = finish(at, groups)
    scores = jnp.sqrt(jnp.sum(squares, axis=1) * (1.0 / (BS * BS)) + EPS)
    return gradients[None, None], scores[None, None]


def solution(mesh):
    in_specs = (P(("blk", "dp"), "team"), P(("blk", "dp"), "team"), P("team", None, None), P())
    out_specs = (P("team", "blk", "dp", None, None), P("team", "blk", "dp"))
    return jax.shard_map(on_device, mesh=mesh, in_specs=in_specs, out_specs=out_specs, check_vma=False)
```
